32 devices in a mesh: groups: 2 (over y), band: 8 (over z, x), blk: 2 (over core).
Axes of the slice: x: 2, y: 2, z: 4, core: 2. Of those that a mesh axis runs over, the one named last changes fastest.
Arguments:
- valence: bfloat16 [256, 4096], P(('groups', 'band')), parts along dimension 0, may hold values from -6 to 6
- conduction: bfloat16 [4096, 128], P('band', ('groups', 'blk')), parts along dimension 1, may hold values from -6 to 6
- val_energy: float32 [256], P(('groups', 'band')), parts along dimension 0, may hold values from -12 to -1
- cond_energy: float32 [128], P(('groups', 'blk')), parts along dimension 0, may hold values from 0.5 to 10
- gvectors: int32 [3, 1024], P(None, 'groups'), parts along dimension 1, may hold values from -8 to 7
Outputs:
- chi: float32 [2, 1024, 512], P(None, ('groups', 'band'), 'blk'), parts along dimension 1
The draws below stay inside these ranges and needn't reach their ends.
There are 2 independent parts, one for each index of `groups`. The reference program is written for one: setup_inputs(seed, part) draws one part's arguments, and reference() takes and returns one part's arrays. A program takes and returns all parts, laid end to end along the dimension named above; each array names one. Nothing has to cross between parts.
All inputs are finite; a program needn't handle non-finite values.
Results may differ from the reference program's by a relative error of at most 0.0037.
Values may be sent and summed in bfloat16 or wider, within the bound.
A program may use at most 64 MiB of HBM per device.

```python
import math
import jax
import jax.numpy as jnp
from jax import lax

VAL_DEV = 16
NC = 64
GRID = 16
GW = 512
NV = 128
NR = 4096


def plant(drawn, own_key, least, largest):
    spot = [jax.random.randint(jax.random.fold_in(own_key, axis), (), 0, length) for axis, length in enumerate(drawn.shape)]
    main_axis = drawn.shape.index(max(drawn.shape))
    beside = spot[:main_axis] + [(spot[main_axis] + 1) % drawn.shape[main_axis]] + spot[main_axis + 1:]
    return drawn.at[tuple(spot)].set(least).at[tuple(beside)].set(largest)


def levels(rng, extent, shards, least, high):
    gain = 1.0
    for axis_at, shards_of in shards:
        draws = jax.random.uniform(jax.random.fold_in(jax.random.fold_in(rng, 6), axis_at), (shards_of,), jnp.float32, least / len(shards), high / len(shards))
        gain = gain * jnp.repeat(jnp.exp(draws), extent[axis_at] // shards_of).reshape((-1,) + (1,) * (len(extent) - 1 - axis_at))
    return gain


def gaussian(stream_key, shape, spread, reach, split=(), kind=jnp.bfloat16):
    gain = levels(stream_key, shape, split, -0.22, 0.18) if split else 1.0
    values = jax.random.normal(stream_key, shape, jnp.float32) * spread * gain
    return jnp.minimum(jnp.maximum(values, -reach), reach).astype(kind)


def setup_inputs(seed: int = 0, part: int = 0) -> dict:
    splits = jax.random.split(jax.random.key(seed), 6)
    own_keys = jax.random.split(jax.random.fold_in(splits[5], part), 6)
    valence = gaussian(own_keys[0], (NV, NR), 1.0, 6.0, ((0, 8),))
    conduction = gaussian(own_keys[1], (NR, NC), 1.0, 6.0, ((0, 8), (1, 2)))
    val_energy = jnp.clip(-12.0 + 11.0 * jax.random.uniform(own_keys[2], (NV,), jnp.float32) ** levels(own_keys[2], (NV,), ((0, 8),), -0.2, 0.2), -12.0, -1.0)
    cond_energy = jnp.clip(0.5 + 9.5 * jax.random.uniform(own_keys[3], (NC,), jnp.float32) ** levels(own_keys[3], (NC,), ((0, 2),), -0.2, 0.2), 0.5, 10.0)
    gvectors = plant(jax.random.randint(own_keys[4], (3, GW), 0 - GRID // 2, GRID // 2), jax.random.fold_in(own_keys[4], 1), 0 - GRID // 2, (GRID // 2) - 1).astype(jnp.int32)
    return dict(valence=valence, conduction=conduction, val_energy=val_energy, cond_energy=cond_energy, gvectors=gvectors)


def make_table(gvectors, grid):
    count = grid * grid * grid
    points = jnp.arange(count, dtype=jnp.int32)
    xs = points // (grid * grid)
    ys = points // grid % grid
    zs = points % grid
    phase_int = xs[:, None] * gvectors[0][None, :] + ys[:, None] * gvectors[1][None, :] + zs[:, None] * gvectors[2][None, :]
    phase_int = jnp.mod(phase_int, grid)
    phase = phase_int.astype(jnp.float32) * (2.0 * math.pi / grid)
    scale = 1.0 / math.sqrt(count)
    return jnp.concatenate([jnp.cos(phase) * scale, -jnp.sin(phase) * scale], axis=1).astype(jnp.bfloat16)

def chi_block(weighted, elements, width):
    dims = (((0,), (0,)), ((), ()))
    left_re = weighted[:, :width]
    left_im = weighted[:, width:]
    right_re = elements[:, :width]
    right_im = elements[:, width:]
    real_part = lax.dot_general(left_re, right_re, dims, preferred_element_type=jnp.float32) + lax.dot_general(left_im, right_im, dims, preferred_element_type=jnp.float32)
    imag_part = lax.dot_general(left_im, right_re, dims, preferred_element_type=jnp.float32) - lax.dot_general(left_re, right_im, dims, preferred_element_type=jnp.float32)
    return jnp.stack([real_part, imag_part])

def reference(valence, conduction, val_energy, cond_energy, gvectors):
    table = make_table(gvectors, GRID)
    norm = 1.0 / math.sqrt(NV * NC)
    blocks = NV // VAL_DEV
    val_blocks = valence.reshape(blocks, VAL_DEV, NR)
    energy_blocks = val_energy.reshape(blocks, VAL_DEV)
    cond_rows = jnp.transpose(conduction).astype(jnp.float32)

    def step(total, item):
        vals, energies = item
        pair = (vals[:, None, :].astype(jnp.float32) * cond_rows[None, :, :]).astype(jnp.bfloat16).reshape(-1, NR)
        elements = jnp.dot(pair, table, preferred_element_type=jnp.float32).astype(jnp.bfloat16)
        factor = (-1.0 / (cond_energy[None, :] - energies[:, None]) * norm).reshape(-1, 1)
        weighted = (elements.astype(jnp.float32) * factor).astype(jnp.bfloat16)
        return (total + chi_block(weighted, elements, GW), None)
    start = jnp.zeros((2, GW, GW), jnp.float32)
    total, unused = lax.scan(step, start, (val_blocks, energy_blocks))
    return total
```

```python
import functools
import math

import jax
import jax.numpy as jnp
from jax import lax
from jax.experimental import pallas as pl
from jax.experimental.pallas import tpu as pltpu
from jax.sharding import PartitionSpec as P

GRID = 16
F32 = jnp.float32
BF16 = jnp.bfloat16
NT = (((1,), (1,)), ((), ()))


def cos_sin(theta):
    t = theta * theta
    cos = jnp.full_like(t, 1.0 / math.factorial(16))
    for n in range(14, -1, -2):
        cos = cos * t + (-1.0) ** (n // 2) / math.factorial(n)
    sin = jnp.full_like(t, 1.0 / math.factorial(17))
    for n in range(15, 0, -2):
        sin = sin * t + (-1.0) ** (n // 2) / math.factorial(n)
    return cos, sin * theta


def unit(phase):
    m = phase - GRID * jnp.floor(phase * (1.0 / GRID))
    cos, sin = cos_sin((m - GRID // 2) * (2.0 * math.pi / GRID))
    return -cos, sin


def chi_kernel(
    n_band, n_blk, val_ref, cond_ref, ve_ref, ce_ref, gv_ref, out_ref,
    gpad, gcol, prot, cond_all, table, pair, acc, wgt, dst_,
    send1, own1, recv1, sendx, recvx, sendz, recvz, sende, recve, other,
    ag_send, ag_fwd, ag_recv, s1_send, s1_recv, sx_send, sx_recv, sz_send, sz_recv, se_send, se_recv,
):
    nz = n_band // 2
    n_val, total_points = val_ref.shape
    block_points, n_cond = cond_ref.shape
    width = gv_ref.shape[1]
    zpoints = 2 * block_points
    plane = GRID * GRID
    xs_per = zpoints // plane
    row_block = width // n_band
    col_block = width // n_blk
    per_blk = col_block // row_block

    b = lax.axis_index("band")
    k = lax.axis_index("blk")
    z = b // 2
    x = b % 2
    xn = b + 1 - 2 * x
    kn = 1 - k

    def dev(band, blk):
        return {"band": band, "blk": blk}

    def zpeer(t):
        return lax.rem(z + t, nz)

    def copy(src, dst, s, r, band, blk):
        return pltpu.make_async_remote_copy(
            src_ref=src, dst_ref=dst, send_sem=s, recv_sem=r,
            device_id=dev(band, blk), device_id_type=pl.DeviceIdType.MESH,
        )

    barrier = pltpu.get_barrier_semaphore()

    def greet(band, blk):
        pl.semaphore_signal(barrier, inc=1, device_id=dev(band, blk), device_id_type=pl.DeviceIdType.MESH)

    greet(b, kn)
    greet(xn, k)
    for t in range(1, nz):
        greet(zpeer(t) * 2 + x, k)
    mirror_blk = b // per_blk
    for j in range(per_blk):
        @pl.when(k * per_blk + j != b)
        def _():
            greet(k * per_blk + j, mirror_blk)

    eye = (
        lax.broadcasted_iota(jnp.int32, (n_cond, n_cond), 0) == lax.broadcasted_iota(jnp.int32, (n_cond, n_cond), 1)
    ).astype(F32).astype(BF16)
    cond_all[b] = lax.dot_general(eye, cond_ref[...], NT, preferred_element_type=F32).astype(BF16)

    pl.semaphore_wait(barrier, 1 + nz + per_blk - jnp.where(mirror_blk == k, 1, 0))

    sends = []
    for t in range(1, nz):
        c = copy(cond_all.at[b], cond_all.at[b], ag_send.at[t], ag_recv.at[b], zpeer(t) * 2 + x, k)
        c.start()
        sends.append(c)
    c = copy(cond_all.at[b], cond_all.at[b], ag_send.at[0], ag_recv.at[b], xn, k)
    c.start()
    sends.append(c)

    gpad[...] = jnp.zeros_like(gpad)
    gpad[0:3, :] = gv_ref[...].astype(F32)
    gcol[...] = jnp.transpose(gpad[...])
    lane = lax.broadcasted_iota(jnp.int32, (1, 128), 1).astype(F32)
    pc, ps = unit(gcol[:, 0:1] * lane)
    prot[0] = pc
    prot[1] = ps
    tile = 32
    inplane = lax.broadcasted_iota(jnp.int32, (1, plane), 1)
    ys = (inplane // GRID).astype(F32)
    zs = (inplane % GRID).astype(F32)
    scale = 1.0 / math.sqrt(total_points)

    def table_tile(i, carry):
        rows = pl.ds(pl.multiple_of(i * tile, tile), tile)
        rows_im = pl.ds(pl.multiple_of(width + i * tile, tile), tile)
        g = gcol[rows, :]
        qc, qs = unit(g[:, 1:2] * ys + g[:, 2:3] * zs)
        qc = qc * scale
        qs = qs * scale
        pc = prot[0, rows, :]
        ps = prot[1, rows, :]
        for xx in range(GRID):
            cp = pc[:, xx : xx + 1]
            sp = ps[:, xx : xx + 1]
            cols = slice((xx % xs_per) * plane, (xx % xs_per + 1) * plane)
            table[xx // xs_per, rows, cols] = (cp * qc - sp * qs).astype(BF16)
            table[xx // xs_per, rows_im, cols] = (sp * qc + cp * qs).astype(BF16)
        return carry

    lax.fori_loop(0, width // tile, table_tile, 0)

    for t in range(1, nz):
        slot = zpeer(t) * 2 + x
        c = copy(cond_all.at[slot], cond_all.at[slot], ag_fwd.at[t], ag_recv.at[slot], xn, k)
        c.wait_recv()
        c.start()
        sends.append(c)

    def step(t, carry):
        zz = zpeer(t)
        near = zz * 2 + x
        far = zz * 2 + 1 - x
        copy(cond_all.at[far], cond_all.at[far], ag_send.at[0], ag_recv.at[far], xn, k).wait_recv()
        for h in range(2):
            conds = cond_all[zz * 2 + h].astype(F32)
            start = pl.multiple_of((zz * 2 + h) * block_points, block_points)
            vals = val_ref[:, pl.ds(start, block_points)].astype(F32)
            for v in range(n_val):
                pair[v * n_cond : (v + 1) * n_cond, h * block_points : (h + 1) * block_points] = (
                    conds * vals[v : v + 1, :]
                ).astype(BF16)

        def rows_of(i, c):
            rows = pl.ds(pl.multiple_of(i * 256, 256), 256)
            part = lax.dot_general(table[zz, rows, :], pair[...], NT, preferred_element_type=F32)

            @pl.when(t == 0)
            def _():
                acc[rows, :] = part

            @pl.when(t > 0)
            def _():
                acc[rows, :] += part

            return c

        lax.fori_loop(0, 2 * width // 256, rows_of, 0)
        return carry

    lax.fori_loop(0, nz, step, 0)

    n_pair = n_val * n_cond
    pos = lax.broadcasted_iota(jnp.int32, (1, n_pair), 1)
    ve_row = jnp.zeros((1, n_pair), F32)
    for v in range(n_val):
        ve_row = jnp.where(pos // n_cond == v, ve_ref[v], ve_row)
    ce_row = jnp.zeros((1, n_pair), F32)
    for c in range(n_cond):
        ce_row = jnp.where(pos % n_cond == c, ce_ref[c], ce_row)
    norm = 1.0 / math.sqrt(n_val * n_band * n_cond * n_blk)
    factor = -1.0 / (ce_row - ve_row) * norm

    ctile = 64

    def weigh(i, carry):
        rows = pl.ds(pl.multiple_of(i * ctile, ctile), ctile)
        rows_im = pl.ds(pl.multiple_of(width + i * ctile, ctile), ctile)
        a = acc[rows, :].astype(BF16).astype(F32)
        bb = acc[rows_im, :].astype(BF16).astype(F32)
        wgt[rows, 0:n_pair] = (a * factor).astype(BF16)
        wgt[rows, n_pair : 2 * n_pair] = (bb * factor).astype(BF16)
        dst_[rows, 0:n_pair] = (a - bb).astype(BF16)
        dst_[rows, n_pair : 2 * n_pair] = (a + bb).astype(BF16)
        return carry

    lax.fori_loop(0, width // ctile, weigh, 0)

    def half(blk):
        cols = pl.ds(pl.multiple_of(blk * col_block, col_block), col_block)
        return lax.dot_general(wgt[...], dst_[cols, :], NT, preferred_element_type=F32)

    theirs = half(kn)
    for i in range(n_band):
        send1[i % 2, i // 2] = theirs[i * row_block : (i + 1) * row_block, :].astype(BF16)
    first = copy(send1.at[1 - x], recv1.at[1 - x], s1_send.at[0], s1_recv.at[0], b, kn)
    second = copy(send1.at[x], recv1.at[x], s1_send.at[1], s1_recv.at[1], b, kn)
    first.start()
    second.start()
    mine = half(k)
    for i in range(n_band):
        own1[i % 2, i // 2] = mine[i * row_block : (i + 1) * row_block, :]

    first.wait_recv()
    xcopies = []
    for t in list(range(1, nz)) + [0]:
        zz = zpeer(t)
        sendx[zz] = (own1[1 - x, zz] + recv1[1 - x, zz].astype(F32)).astype(BF16)
        c = copy(sendx.at[zz], recvx.at[zz], sx_send.at[zz], sx_recv.at[zz], xn, k)
        c.start()
        xcopies.append(c)
    second.wait_recv()

    zcopies = []
    for i, t in enumerate(list(range(1, nz)) + [0]):
        zz = zpeer(t)
        xcopies[i].wait_recv()
        total = own1[x, zz] + recv1[x, zz].astype(F32) + recvx[zz].astype(F32)
        if t == 0:
            final = total
        else:
            sendz[zz] = total.astype(BF16)
            c = copy(sendz.at[zz], recvz.at[z], sz_send.at[zz], sz_recv.at[z], zz * 2 + x, k)
            c.start()
            zcopies.append(c)
    for t in range(1, nz):
        zz = zpeer(t)
        copy(sendz.at[zz], recvz.at[zz], sz_send.at[zz], sz_recv.at[zz], zz * 2 + x, k).wait_recv()
        final = final + recvz[zz].astype(F32)

    packed_rows = row_block // 2
    place = lax.rem(b, per_blk)
    for j in range(per_blk):
        block = final[:, j * row_block : (j + 1) * row_block]
        sende[j] = jnp.concatenate([block[:packed_rows], block[packed_rows:]], axis=1).astype(BF16)

        @pl.when(k * per_blk + j != b)
        def _():
            copy(sende.at[j], recve.at[place], se_send.at[j], se_recv.at[place], k * per_blk + j, mirror_blk).start()

        @pl.when(k * per_blk + j == b)
        def _():
            other[j * row_block : (j + 1) * row_block, :] = block

    for j in range(per_blk):
        @pl.when(k * per_blk + j != b)
        def _():
            copy(sende.at[j], recve.at[j], se_send.at[j], se_recv.at[j], k * per_blk + j, mirror_blk).wait_recv()
            got = recve[j].astype(F32)
            other[j * row_block : j * row_block + packed_rows, :] = got[:, :row_block]
            other[j * row_block + packed_rows : (j + 1) * row_block, :] = got[:, row_block:]

    mirror = jnp.transpose(other[...])
    out_ref[0] = (final + mirror) * 0.5
    out_ref[1] = (final - mirror) * 0.5

    for c in sends + xcopies + zcopies + [first, second]:
        c.wait_send()
    for j in range(per_blk):
        @pl.when(k * per_blk + j != b)
        def _():
            copy(sende.at[j], recve.at[j], se_send.at[j], se_recv.at[j], k * per_blk + j, mirror_blk).wait_send()


def fused(valence, conduction, val_energy, cond_energy, gvectors):
    n_band = lax.axis_size("band")
    n_blk = lax.axis_size("blk")
    nz = n_band // 2
    n_val, total_points = valence.shape
    block_points, n_cond = conduction.shape
    width = gvectors.shape[1]
    row_block = width // n_band
    col_block = width // n_blk
    per_blk = col_block // row_block
    n_pair = n_val * n_cond
    dma = pltpu.SemaphoreType.DMA
    vmem = pl.BlockSpec(memory_space=pltpu.VMEM)
    smem = pl.BlockSpec(memory_space=pltpu.SMEM)
    return pl.pallas_call(
        functools.partial(chi_kernel, n_band, n_blk),
        out_shape=jax.ShapeDtypeStruct((2, row_block, col_block), F32),
        in_specs=[vmem, vmem, smem, smem, vmem],
        out_specs=vmem,
        scratch_shapes=[
            pltpu.VMEM((8, width), F32),
            pltpu.VMEM((width, 8), F32),
            pltpu.VMEM((2, width, 128), F32),
            pltpu.VMEM((n_band, n_cond, block_points), BF16),
            pltpu.VMEM((nz, 2 * width, 2 * block_points), BF16),
            pltpu.VMEM((n_pair, 2 * block_points), BF16),
            pltpu.VMEM((2 * width, n_pair), F32),
            pltpu.VMEM((width, 2 * n_pair), BF16),
            pltpu.VMEM((width, 2 * n_pair), BF16),
            pltpu.VMEM((2, nz, row_block, col_block), BF16),
            pltpu.VMEM((2, nz, row_block, col_block), F32),
            pltpu.VMEM((2, nz, row_block, col_block), BF16),
            pltpu.VMEM((nz, row_block, col_block), BF16),
            pltpu.VMEM((nz, row_block, col_block), BF16),
            pltpu.VMEM((nz, row_block, col_block), BF16),
            pltpu.VMEM((nz, row_block, col_block), BF16),
            pltpu.VMEM((per_blk, row_block // 2, 2 * row_block), BF16),
            pltpu.VMEM((per_blk, row_block // 2, 2 * row_block), BF16),
            pltpu.VMEM((col_block, row_block), F32),
            dma((nz,)), dma((nz,)), dma((n_band,)), dma((2,)), dma((2,)),
            dma((nz,)), dma((nz,)), dma((nz,)), dma((nz,)), dma((per_blk,)), dma((per_blk,)),
        ],
        compiler_params=pltpu.CompilerParams(
            collective_id=0, has_side_effects=True, vmem_limit_bytes=48 * 2**20
        ),
    )(valence, conduction, val_energy, cond_energy, gvectors)


def table_rows(gvectors, grid, start, count):
    total_points = grid * grid * grid
    points = start + jnp.arange(count, dtype=jnp.int32)
    xs = points // (grid * grid)
    ys = points // grid % grid
    zs = points % grid
    phase_int = (
        xs[:, None] * gvectors[0][None, :]
        + ys[:, None] * gvectors[1][None, :]
        + zs[:, None] * gvectors[2][None, :]
    )
    phase_int = jnp.mod(phase_int, grid)
    phase = phase_int.astype(jnp.float32) * (2.0 * math.pi / grid)
    scale = 1.0 / math.sqrt(total_points)
    return jnp.concatenate([jnp.cos(phase) * scale, -jnp.sin(phase) * scale], axis=1).astype(
        jnp.bfloat16
    )


def chi_part(weighted, elements, width, row_start, row_count, col_start, col_count):
    dims = (((0,), (0,)), ((), ()))
    left_re = lax.dynamic_slice_in_dim(weighted, row_start, row_count, 1)
    left_im = lax.dynamic_slice_in_dim(weighted, row_start + width, row_count, 1)
    right_re = lax.dynamic_slice_in_dim(elements, col_start, col_count, 1)
    right_im = lax.dynamic_slice_in_dim(elements, col_start + width, col_count, 1)
    real_part = lax.dot_general(
        left_re, right_re, dims, preferred_element_type=jnp.float32
    ) + lax.dot_general(left_im, right_im, dims, preferred_element_type=jnp.float32)
    imag_part = lax.dot_general(
        left_im, right_re, dims, preferred_element_type=jnp.float32
    ) - lax.dot_general(left_re, right_im, dims, preferred_element_type=jnp.float32)
    return (real_part, imag_part)


def per_device(valence, conduction, val_energy, cond_energy, gvectors):
    width = gvectors.shape[1]
    val_count = valence.shape[0]
    cond_count = conduction.shape[1]
    n_band = lax.axis_size("band")
    n_blk = lax.axis_size("blk")
    row_block = width // n_band
    col_block = width // n_blk
    points_all = valence.shape[1]
    point_block = min(512, points_all)
    gathered = lax.all_gather(conduction, "band", axis=0, tiled=True)
    cond_rows = jnp.transpose(gathered).astype(jnp.float32)
    summed = jnp.zeros((val_count * cond_count, 2 * width), jnp.float32)
    for block_index in range(points_all // point_block):
        start = block_index * point_block
        vals = valence[:, start : start + point_block].astype(jnp.float32)
        conds = cond_rows[:, start : start + point_block]
        pair = (vals[:, None, :] * conds[None, :, :]).astype(jnp.bfloat16).reshape(-1, point_block)
        tab_block = table_rows(gvectors, GRID, start, point_block)
        summed = summed + jnp.dot(pair, tab_block, preferred_element_type=jnp.float32)
    elements = summed.astype(jnp.bfloat16)
    val_total = val_count * n_band
    cond_total = cond_count * n_blk
    norm = 1.0 / math.sqrt(val_total * cond_total)
    factor = (-1.0 / (cond_energy[None, :] - val_energy[:, None]) * norm).reshape(-1, 1)
    weighted = (elements.astype(jnp.float32) * factor).astype(jnp.bfloat16)
    band_index = lax.axis_index("band")
    blk_index = lax.axis_index("blk")
    real_part, imag_part = chi_part(weighted, elements, width, 0, width, 0, width)
    total = lax.psum(jnp.stack([real_part, imag_part]), ("band", "blk"))
    mine = lax.dynamic_slice_in_dim(total, band_index * row_block, row_block, 1)
    return lax.dynamic_slice_in_dim(mine, blk_index * col_block, col_block, 2)


def fits(mesh, valence, conduction, gvectors):
    n_band, n_blk, parts = mesh.shape["band"], mesh.shape["blk"], mesh.shape["groups"]
    width = gvectors.shape[1] // parts
    return (
        n_blk == 2 and n_band % 2 == 0 and n_band <= 16 and n_band % n_blk == 0
        and width // n_band == 64 and valence.shape[1] == GRID**3
        and conduction.shape[0] // n_band % (GRID * GRID) == 0
        and conduction.shape[1] // (parts * n_blk) % 16 == 0
    )


def solution(mesh):
    in_specs = (
        P(("groups", "band"), None),
        P("band", ("groups", "blk")),
        P(("groups", "band")),
        P(("groups", "blk")),
        P(None, "groups"),
    )
    out_specs = P(None, ("groups", "band"), "blk")

    def run(valence, conduction, val_energy, cond_energy, gvectors):
        body = fused if fits(mesh, valence, conduction, gvectors) else per_device
        return jax.shard_map(
            body, mesh=mesh, in_specs=in_specs, out_specs=out_specs, check_vma=False
        )(valence, conduction, val_energy, cond_energy, gvectors)

    return run
```

```python
import functools
import math

import jax
import jax.numpy as jnp
from jax import lax
from jax.experimental import pallas as pl
from jax.experimental.pallas import tpu as pltpu
from jax.sharding import PartitionSpec as P

GRID = 16
F32 = jnp.float32
BF16 = jnp.bfloat16
NT = (((1,), (1,)), ((), ()))


def cos_sin(theta):
    t = theta * theta
    cos = jnp.full_like(t, 1.0 / math.factorial(16))
    for n in range(14, -1, -2):
        cos = cos * t + (-1.0) ** (n // 2) / math.factorial(n)
    sin = jnp.full_like(t, 1.0 / math.factorial(17))
    for n in range(15, 0, -2):
        sin = sin * t + (-1.0) ** (n // 2) / math.factorial(n)
    return cos, sin * theta


def unit(phase):
    m = phase - GRID * jnp.floor(phase * (1.0 / GRID))
    cos, sin = cos_sin((m - GRID // 2) * (2.0 * math.pi / GRID))
    return -cos, sin


def chi_kernel(
    n_band, n_blk, val_hbm, cond_hbm, ve_hbm, ce_hbm, gv_hbm, out_ref,
    val_ref, ve_ref, ce_ref, gv_ref,
    gpad, gcol, prot, cond_all, table, pair, acc, wgt, dst_,
    send1, own1, recv1, sendx, recvx, sendz, recvz, sende, recve, other,
    in_sem, ag_send, ag_fwd, ag_recv, s1_send, s1_recv, sx_send, sx_recv, sz_send, sz_recv, se_send, se_recv,
):
    nz = n_band // 2
    n_val, total_points = val_hbm.shape
    n_cond, block_points = cond_hbm.shape
    width = gv_hbm.shape[1]
    plane = GRID * GRID
    xs_per = block_points // plane
    row_block = width // n_band
    col_block = width // n_blk
    per_blk = col_block // row_block

    b = lax.axis_index("band")
    k = lax.axis_index("blk")
    z = b // 2
    x = b % 2
    xn = b + 1 - 2 * x
    kn = 1 - k

    def dev(band, blk):
        return {"band": band, "blk": blk}

    def zpeer(t):
        return lax.rem(z + t, nz)

    def copy(src, dst, s, r, band, blk):
        return pltpu.make_async_remote_copy(
            src_ref=src, dst_ref=dst, send_sem=s, recv_sem=r,
            device_id=dev(band, blk), device_id_type=pl.DeviceIdType.MESH,
        )

    barrier = pltpu.get_barrier_semaphore()

    def greet(band, blk):
        pl.semaphore_signal(barrier, inc=1, device_id=dev(band, blk), device_id_type=pl.DeviceIdType.MESH)

    greet(b, kn)
    greet(xn, k)
    for t in range(1, nz):
        greet(zpeer(t) * 2 + x, k)
    mirror_blk = b // per_blk
    for j in range(per_blk):
        @pl.when(k * per_blk + j != b)
        def _():
            greet(k * per_blk + j, mirror_blk)

    cond_ref = cond_all.at[b]
    loads = [
        pltpu.make_async_copy(src, dst, in_sem.at[i])
        for i, (src, dst) in enumerate(
            [(gv_hbm, gv_ref), (cond_hbm, cond_ref), (val_hbm, val_ref), (ve_hbm, ve_ref), (ce_hbm, ce_ref)]
        )
    ]
    for c in loads:
        c.start()
    loads[0].wait()

    pl.semaphore_wait(barrier, 1 + nz + per_blk - jnp.where(mirror_blk == k, 1, 0))

    for c in loads[1:]:
        c.wait()
    sends = []
    c = copy(cond_ref, cond_all.at[b], ag_send.at[0], ag_recv.at[b], xn, k)
    c.start()
    sends.append(c)
    for t in range(1, nz):
        c = copy(cond_ref, cond_all.at[b], ag_send.at[t], ag_recv.at[b], zpeer(t) * 2 + x, k)
        c.start()
        sends.append(c)

    gpad[...] = jnp.zeros_like(gpad)
    gpad[0:3, :] = gv_ref[...].astype(F32)
    gcol[...] = jnp.transpose(gpad[...])
    lane = lax.broadcasted_iota(jnp.int32, (1, 128), 1).astype(F32)
    pc, ps = unit(gcol[:, 0:1] * lane)
    prot[0] = pc
    prot[1] = ps
    tile = 32
    inplane = lax.broadcasted_iota(jnp.int32, (1, plane), 1)
    ys = (inplane // GRID).astype(F32)
    zs = (inplane % GRID).astype(F32)
    scale = 1.0 / math.sqrt(total_points)

    def table_tile(i, carry):
        rows = pl.ds(pl.multiple_of(i * tile, tile), tile)
        rows_im = pl.ds(pl.multiple_of(width + i * tile, tile), tile)
        g = gcol[rows, :]
        qc, qs = unit(g[:, 1:2] * ys + g[:, 2:3] * zs)
        qc = qc * scale
        qs = qs * scale
        pc = prot[0, rows, :]
        ps = prot[1, rows, :]
        flip = jnp.broadcast_to(pc[:, GRID // 2 : GRID // 2 + 1], (tile, plane)).astype(BF16)
        for xx in range(GRID // 2):
            cp = pc[:, xx : xx + 1]
            sp = ps[:, xx : xx + 1]
            re = (cp * qc - sp * qs).astype(BF16)
            im = (sp * qc + cp * qs).astype(BF16)
            for at, r, m in ((xx, re, im), (xx + GRID // 2, re * flip, im * flip)):
                cols = slice((at % xs_per) * plane, (at % xs_per + 1) * plane)
                table[at // xs_per, rows, cols] = r
                table[at // xs_per, rows_im, cols] = m
        return carry

    lax.fori_loop(0, width // tile, table_tile, 0)

    def arrived(slot):
        copy(cond_all.at[slot], cond_all.at[slot], ag_send.at[0], ag_recv.at[slot], xn, k).wait_recv()

    def accumulate(blocks, first):
        for i, (slot, conds) in enumerate(blocks):
            conds = conds[...].astype(F32)
            start = pl.multiple_of(slot * block_points, block_points)
            vals = val_ref[:, pl.ds(start, block_points)].astype(F32)
            for v in range(n_val):
                pair[i, v * n_cond : (v + 1) * n_cond, :] = (conds * vals[v : v + 1, :]).astype(BF16)

        def rows_of(r, carry):
            rows = pl.ds(pl.multiple_of(r * dot_rows, dot_rows), dot_rows)
            part = None
            for i, (slot, _) in enumerate(blocks):
                term = lax.dot_general(table[slot, rows, :], pair[i], NT, preferred_element_type=F32)
                part = term if part is None else part + term
            if first:
                acc[rows, :] = part
            else:
                acc[rows, :] += part
            return carry

        lax.fori_loop(0, 2 * width // dot_rows, rows_of, 0)

    dot_rows = 2 * width

    near = []
    far = []
    for t in range(1, nz):
        slot = zpeer(t) * 2 + x
        arrived(slot)
        c = copy(cond_all.at[slot], cond_all.at[slot], ag_fwd.at[t], ag_recv.at[slot], xn, k)
        c.start()
        sends.append(c)
        near.append((slot, cond_all.at[slot]))
        far.append((zpeer(t) * 2 + 1 - x, cond_all.at[zpeer(t) * 2 + 1 - x]))
    arrived(xn)
    accumulate([(b, cond_ref), (xn, cond_all.at[xn])] + near, True)
    for slot, _ in far:
        arrived(slot)
    accumulate(far, False)

    n_pair = n_val * n_cond
    pos = lax.broadcasted_iota(jnp.int32, (1, n_pair), 1)
    ve_row = jnp.zeros((1, n_pair), F32)
    for v in range(n_val):
        ve_row = jnp.where(pos // n_cond == v, ve_ref[v], ve_row)
    ce_row = jnp.zeros((1, n_pair), F32)
    for c in range(n_cond):
        ce_row = jnp.where(pos % n_cond == c, ce_ref[c], ce_row)
    norm = 1.0 / math.sqrt(n_val * n_band * n_cond * n_blk)
    factor = -1.0 / (ce_row - ve_row) * norm

    ctile = 64

    def weigh(i, carry):
        rows = pl.ds(pl.multiple_of(i * ctile, ctile), ctile)
        rows_im = pl.ds(pl.multiple_of(width + i * ctile, ctile), ctile)
        a = acc[rows, :].astype(BF16).astype(F32)
        bb = acc[rows_im, :].astype(BF16).astype(F32)
        wgt[rows, 0:n_pair] = (a * factor).astype(BF16)
        wgt[rows, n_pair : 2 * n_pair] = (bb * factor).astype(BF16)
        dst_[rows, 0:n_pair] = (a - bb).astype(BF16)
        dst_[rows, n_pair : 2 * n_pair] = (a + bb).astype(BF16)
        return carry

    lax.fori_loop(0, width // ctile, weigh, 0)

    def half(blk):
        cols = pl.ds(pl.multiple_of(blk * col_block, col_block), col_block)
        return lax.dot_general(wgt[...], dst_[cols, :], NT, preferred_element_type=F32)

    theirs = half(kn)
    for i in range(n_band):
        send1[i % 2, i // 2] = theirs[i * row_block : (i + 1) * row_block, :].astype(BF16)
    first = copy(send1.at[1 - x], recv1.at[1 - x], s1_send.at[0], s1_recv.at[0], b, kn)
    second = copy(send1.at[x], recv1.at[x], s1_send.at[1], s1_recv.at[1], b, kn)
    first.start()
    second.start()
    mine = half(k)
    for i in range(n_band):
        own1[i % 2, i // 2] = mine[i * row_block : (i + 1) * row_block, :]

    first.wait_recv()
    xcopies = []
    for t in list(range(1, nz)) + [0]:
        zz = zpeer(t)
        sendx[zz] = (own1[1 - x, zz] + recv1[1 - x, zz].astype(F32)).astype(BF16)
        c = copy(sendx.at[zz], recvx.at[zz], sx_send.at[zz], sx_recv.at[zz], xn, k)
        c.start()
        xcopies.append(c)
    second.wait_recv()

    zcopies = []
    for i, t in enumerate(list(range(1, nz)) + [0]):
        zz = zpeer(t)
        xcopies[i].wait_recv()
        total = own1[x, zz] + recv1[x, zz].astype(F32) + recvx[zz].astype(F32)
        if t == 0:
            final = total
        else:
            sendz[zz] = total.astype(BF16)
            c = copy(sendz.at[zz], recvz.at[z], sz_send.at[zz], sz_recv.at[z], zz * 2 + x, k)
            c.start()
            zcopies.append(c)
    for t in range(1, nz):
        zz = zpeer(t)
        copy(sendz.at[zz], recvz.at[zz], sz_send.at[zz], sz_recv.at[zz], zz * 2 + x, k).wait_recv()
        final = final + recvz[zz].astype(F32)

    packed_rows = row_block // 2
    place = lax.rem(b, per_blk)
    for j in range(per_blk):
        block = final[:, j * row_block : (j + 1) * row_block]
        sende[j] = jnp.concatenate([block[:packed_rows], block[packed_rows:]], axis=1).astype(BF16)

        @pl.when(k * per_blk + j != b)
        def _():
            copy(sende.at[j], recve.at[place], se_send.at[j], se_recv.at[place], k * per_blk + j, mirror_blk).start()

        @pl.when(k * per_blk + j == b)
        def _():
            other[j * row_block : (j + 1) * row_block, :] = block

    for j in range(per_blk):
        @pl.when(k * per_blk + j != b)
        def _():
            copy(sende.at[j], recve.at[j], se_send.at[j], se_recv.at[j], k * per_blk + j, mirror_blk).wait_recv()
            got = recve[j].astype(F32)
            other[j * row_block : j * row_block + packed_rows, :] = got[:, :row_block]
            other[j * row_block + packed_rows : (j + 1) * row_block, :] = got[:, row_block:]

    mirror = jnp.transpose(other[...])
    out_ref[0] = (final + mirror) * 0.5
    out_ref[1] = (final - mirror) * 0.5

    for c in sends + xcopies + zcopies + [first, second]:
        c.wait_send()
    for j in range(per_blk):
        @pl.when(k * per_blk + j != b)
        def _():
            copy(sende.at[j], recve.at[j], se_send.at[j], se_recv.at[j], k * per_blk + j, mirror_blk).wait_send()


def fused(valence, conduction, val_energy, cond_energy, gvectors):
    n_band = lax.axis_size("band")
    n_blk = lax.axis_size("blk")
    nz = n_band // 2
    n_val, total_points = valence.shape
    block_points, n_cond = conduction.shape
    width = gvectors.shape[1]
    row_block = width // n_band
    col_block = width // n_blk
    per_blk = col_block // row_block
    n_pair = n_val * n_cond
    dma = pltpu.SemaphoreType.DMA
    vmem = pl.BlockSpec(memory_space=pltpu.VMEM)
    return pl.pallas_call(
        functools.partial(chi_kernel, n_band, n_blk),
        out_shape=jax.ShapeDtypeStruct((2, row_block, col_block), F32),
        in_specs=[pl.BlockSpec(memory_space=pltpu.HBM)] * 5,
        out_specs=vmem,
        scratch_shapes=[
            pltpu.VMEM(valence.shape, BF16),
            pltpu.SMEM(val_energy.shape, F32),
            pltpu.SMEM(cond_energy.shape, F32),
            pltpu.VMEM(gvectors.shape, jnp.int32),
            pltpu.VMEM((8, width), F32),
            pltpu.VMEM((width, 8), F32),
            pltpu.VMEM((2, width, 128), F32),
            pltpu.VMEM((n_band, n_cond, block_points), BF16),
            pltpu.VMEM((n_band, 2 * width, block_points), BF16),
            pltpu.VMEM((nz + 1, n_pair, block_points), BF16),
            pltpu.VMEM((2 * width, n_pair), F32),
            pltpu.VMEM((width, 2 * n_pair), BF16),
            pltpu.VMEM((width, 2 * n_pair), BF16),
            pltpu.VMEM((2, nz, row_block, col_block), BF16),
            pltpu.VMEM((2, nz, row_block, col_block), F32),
            pltpu.VMEM((2, nz, row_block, col_block), BF16),
            pltpu.VMEM((nz, row_block, col_block), BF16),
            pltpu.VMEM((nz, row_block, col_block), BF16),
            pltpu.VMEM((nz, row_block, col_block), BF16),
            pltpu.VMEM((nz, row_block, col_block), BF16),
            pltpu.VMEM((per_blk, row_block // 2, 2 * row_block), BF16),
            pltpu.VMEM((per_blk, row_block // 2, 2 * row_block), BF16),
            pltpu.VMEM((col_block, row_block), F32),
            dma((5,)), dma((nz,)), dma((nz,)), dma((n_band,)), dma((2,)), dma((2,)),
            dma((nz,)), dma((nz,)), dma((nz,)), dma((nz,)), dma((per_blk,)), dma((per_blk,)),
        ],
        compiler_params=pltpu.CompilerParams(
            collective_id=0, has_side_effects=True, vmem_limit_bytes=48 * 2**20
        ),
    )(valence, conduction.T, val_energy, cond_energy, gvectors)


def table_rows(gvectors, grid, start, count):
    total_points = grid * grid * grid
    points = start + jnp.arange(count, dtype=jnp.int32)
    xs = points // (grid * grid)
    ys = points // grid % grid
    zs = points % grid
    phase_int = (
        xs[:, None] * gvectors[0][None, :]
        + ys[:, None] * gvectors[1][None, :]
        + zs[:, None] * gvectors[2][None, :]
    )
    phase_int = jnp.mod(phase_int, grid)
    phase = phase_int.astype(jnp.float32) * (2.0 * math.pi / grid)
    scale = 1.0 / math.sqrt(total_points)
    return jnp.concatenate([jnp.cos(phase) * scale, -jnp.sin(phase) * scale], axis=1).astype(
        jnp.bfloat16
    )


def chi_part(weighted, elements, width, row_start, row_count, col_start, col_count):
    dims = (((0,), (0,)), ((), ()))
    left_re = lax.dynamic_slice_in_dim(weighted, row_start, row_count, 1)
    left_im = lax.dynamic_slice_in_dim(weighted, row_start + width, row_count, 1)
    right_re = lax.dynamic_slice_in_dim(elements, col_start, col_count, 1)
    right_im = lax.dynamic_slice_in_dim(elements, col_start + width, col_count, 1)
    real_part = lax.dot_general(
        left_re, right_re, dims, preferred_element_type=jnp.float32
    ) + lax.dot_general(left_im, right_im, dims, preferred_element_type=jnp.float32)
    imag_part = lax.dot_general(
        left_im, right_re, dims, preferred_element_type=jnp.float32
    ) - lax.dot_general(left_re, right_im, dims, preferred_element_type=jnp.float32)
    return (real_part, imag_part)


def per_device(valence, conduction, val_energy, cond_energy, gvectors):
    width = gvectors.shape[1]
    val_count = valence.shape[0]
    cond_count = conduction.shape[1]
    n_band = lax.axis_size("band")
    n_blk = lax.axis_size("blk")
    row_block = width // n_band
    col_block = width // n_blk
    points_all = valence.shape[1]
    point_block = min(512, points_all)
    gathered = lax.all_gather(conduction, "band", axis=0, tiled=True)
    cond_rows = jnp.transpose(gathered).astype(jnp.float32)
    summed = jnp.zeros((val_count * cond_count, 2 * width), jnp.float32)
    for block_index in range(points_all // point_block):
        start = block_index * point_block
        vals = valence[:, start : start + point_block].astype(jnp.float32)
        conds = cond_rows[:, start : start + point_block]
        pair = (vals[:, None, :] * conds[None, :, :]).astype(jnp.bfloat16).reshape(-1, point_block)
        tab_block = table_rows(gvectors, GRID, start, point_block)
        summed = summed + jnp.dot(pair, tab_block, preferred_element_type=jnp.float32)
    elements = summed.astype(jnp.bfloat16)
    val_total = val_count * n_band
    cond_total = cond_count * n_blk
    norm = 1.0 / math.sqrt(val_total * cond_total)
    factor = (-1.0 / (cond_energy[None, :] - val_energy[:, None]) * norm).reshape(-1, 1)
    weighted = (elements.astype(jnp.float32) * factor).astype(jnp.bfloat16)
    band_index = lax.axis_index("band")
    blk_index = lax.axis_index("blk")
    real_part, imag_part = chi_part(weighted, elements, width, 0, width, 0, width)
    total = lax.psum(jnp.stack([real_part, imag_part]), ("band", "blk"))
    mine = lax.dynamic_slice_in_dim(total, band_index * row_block, row_block, 1)
    return lax.dynamic_slice_in_dim(mine, blk_index * col_block, col_block, 2)


def fits(mesh, valence, conduction, gvectors):
    n_band, n_blk, parts = mesh.shape["band"], mesh.shape["blk"], mesh.shape["groups"]
    width = gvectors.shape[1] // parts
    return (
        n_blk == 2 and n_band % 2 == 0 and n_band <= 16 and n_band % n_blk == 0
        and width // n_band == 64 and valence.shape[1] == GRID**3
        and conduction.shape[0] // n_band % (GRID * GRID) == 0
        and conduction.shape[1] // (parts * n_blk) % 16 == 0
    )


def solution(mesh):
    in_specs = (
        P(("groups", "band"), None),
        P("band", ("groups", "blk")),
        P(("groups", "band")),
        P(("groups", "blk")),
        P(None, "groups"),
    )
    out_specs = P(None, ("groups", "band"), "blk")

    def run(valence, conduction, val_energy, cond_energy, gvectors):
        body = fused if fits(mesh, valence, conduction, gvectors) else per_device
        return jax.shard_map(
            body, mesh=mesh, in_specs=in_specs, out_specs=out_specs, check_vma=False
        )(valence, conduction, val_energy, cond_energy, gvectors)

    return run
```

```python
import functools
import math

import jax
import jax.numpy as jnp
from jax import lax
from jax.experimental import pallas as pl
from jax.experimental.pallas import tpu as pltpu
from jax.sharding import PartitionSpec as P

GRID = 16
F32 = jnp.float32
BF16 = jnp.bfloat16
NT = (((1,), (1,)), ((), ()))


def cos_sin(theta):
    t = theta * theta
    cos = jnp.full_like(t, 1.0 / math.factorial(16))
    for n in range(14, -1, -2):
        cos = cos * t + (-1.0) ** (n // 2) / math.factorial(n)
    sin = jnp.full_like(t, 1.0 / math.factorial(17))
    for n in range(15, 0, -2):
        sin = sin * t + (-1.0) ** (n // 2) / math.factorial(n)
    return cos, sin * theta


def unit(phase):
    m = phase - GRID * jnp.floor(phase * (1.0 / GRID))
    cos, sin = cos_sin((m - GRID // 2) * (2.0 * math.pi / GRID))
    return -cos, sin


def chi_kernel(
    n_band, n_blk, val_hbm, cond_hbm, ve_hbm, ce_hbm, gv_hbm, out_ref,
    val_ref, ve_ref, ce_ref, gv_ref,
    gpad, gcol, prot, cond_all, table, pair, acc, wgt, dst_,
    send1, own1, recv1, sendx, recvx, sendz, recvz, sende, recve, other,
    in_sem, ag_send, ag_fwd, ag_recv, s1_send, s1_recv, sx_send, sx_recv, sz_send, sz_recv, se_send, se_recv,
):
    nz = n_band // 2
    n_val, total_points = val_hbm.shape
    n_cond, block_points = cond_hbm.shape
    width = gv_hbm.shape[1]
    plane = GRID * GRID
    xs_per = block_points // plane
    row_block = width // n_band
    col_block = width // n_blk
    per_blk = col_block // row_block

    b = lax.axis_index("band")
    k = lax.axis_index("blk")
    z = b // 2
    x = b % 2
    xn = b + 1 - 2 * x
    kn = 1 - k

    def dev(band, blk):
        return {"band": band, "blk": blk}

    def zpeer(t):
        return lax.rem(z + t, nz)

    def copy(src, dst, s, r, band, blk):
        return pltpu.make_async_remote_copy(
            src_ref=src, dst_ref=dst, send_sem=s, recv_sem=r,
            device_id=dev(band, blk), device_id_type=pl.DeviceIdType.MESH,
        )

    barrier = pltpu.get_barrier_semaphore()

    def greet(band, blk):
        pl.semaphore_signal(barrier, inc=1, device_id=dev(band, blk), device_id_type=pl.DeviceIdType.MESH)

    greet(b, kn)
    greet(xn, k)
    for t in range(1, nz):
        greet(zpeer(t) * 2 + x, k)
    mirror_blk = b // per_blk
    for j in range(per_blk):
        @pl.when(k * per_blk + j != b)
        def _():
            greet(k * per_blk + j, mirror_blk)

    cond_ref = cond_all.at[b]
    loads = [
        pltpu.make_async_copy(src, dst, in_sem.at[i])
        for i, (src, dst) in enumerate(
            [(gv_hbm, gv_ref), (cond_hbm, cond_ref), (val_hbm, val_ref), (ve_hbm, ve_ref), (ce_hbm, ce_ref)]
        )
    ]
    for c in loads:
        c.start()
    loads[0].wait()

    gpad[...] = jnp.zeros_like(gpad)
    gpad[0:3, :] = gv_ref[...].astype(F32)
    gcol[...] = jnp.transpose(gpad[...])
    lane = lax.broadcasted_iota(jnp.int32, (1, 128), 1).astype(F32)
    pc, ps = unit(gcol[:, 0:1] * lane)
    prot[0] = pc
    prot[1] = ps
    tile = 32
    inplane = lax.broadcasted_iota(jnp.int32, (1, plane), 1)
    ys = (inplane // GRID).astype(F32)
    zs = (inplane % GRID).astype(F32)
    scale = 1.0 / math.sqrt(total_points)

    def table_tile(i, carry):
        rows = pl.ds(pl.multiple_of(i * tile, tile), tile)
        rows_im = pl.ds(pl.multiple_of(width + i * tile, tile), tile)
        g = gcol[rows, :]
        qc, qs = unit(g[:, 1:2] * ys + g[:, 2:3] * zs)
        qc = qc * scale
        qs = qs * scale
        pc = prot[0, rows, :]
        ps = prot[1, rows, :]
        flip = jnp.broadcast_to(pc[:, GRID // 2 : GRID // 2 + 1], (tile, plane)).astype(BF16)
        for xx in range(GRID // 2):
            cp = pc[:, xx : xx + 1]
            sp = ps[:, xx : xx + 1]
            re = (cp * qc - sp * qs).astype(BF16)
            im = (sp * qc + cp * qs).astype(BF16)
            for at, r, m in ((xx, re, im), (xx + GRID // 2, re * flip, im * flip)):
                cols = slice((at % xs_per) * plane, (at % xs_per + 1) * plane)
                table[at // xs_per, rows, cols] = r
                table[at // xs_per, rows_im, cols] = m
        return carry

    lax.fori_loop(0, width // tile // 2, table_tile, 0)
    pl.semaphore_wait(barrier, 1 + nz + per_blk - jnp.where(mirror_blk == k, 1, 0))

    for c in loads[1:]:
        c.wait()
    sends = []
    c = copy(cond_ref, cond_all.at[b], ag_send.at[0], ag_recv.at[b], xn, k)
    c.start()
    sends.append(c)
    for t in range(1, nz):
        c = copy(cond_ref, cond_all.at[b], ag_send.at[t], ag_recv.at[b], zpeer(t) * 2 + x, k)
        c.start()
        sends.append(c)

    lax.fori_loop(width // tile // 2, width // tile, table_tile, 0)

    def arrived(slot):
        copy(cond_all.at[slot], cond_all.at[slot], ag_send.at[0], ag_recv.at[slot], xn, k).wait_recv()

    def accumulate(blocks, first):
        for i, (slot, conds) in enumerate(blocks):
            conds = conds[...].astype(F32)
            start = pl.multiple_of(slot * block_points, block_points)
            vals = val_ref[:, pl.ds(start, block_points)].astype(F32)
            for v in range(n_val):
                pair[i, v * n_cond : (v + 1) * n_cond, :] = (conds * vals[v : v + 1, :]).astype(BF16)

        def rows_of(r, carry):
            rows = pl.ds(pl.multiple_of(r * dot_rows, dot_rows), dot_rows)
            part = None
            for i, (slot, _) in enumerate(blocks):
                term = lax.dot_general(table[slot, rows, :], pair[i], NT, preferred_element_type=F32)
                part = term if part is None else part + term
            if first:
                acc[rows, :] = part
            else:
                acc[rows, :] += part
            return carry

        for r in range(2 * width // dot_rows):
            rows_of(r, 0)

    dot_rows = 512

    accumulate([(b, cond_ref)], True)

    near = []
    far = []
    for t in range(1, nz):
        slot = zpeer(t) * 2 + x
        arrived(slot)
        c = copy(cond_all.at[slot], cond_all.at[slot], ag_fwd.at[t], ag_recv.at[slot], xn, k)
        c.start()
        sends.append(c)
        near.append((slot, cond_all.at[slot]))
        far.append((zpeer(t) * 2 + 1 - x, cond_all.at[zpeer(t) * 2 + 1 - x]))
    arrived(xn)
    accumulate([(xn, cond_all.at[xn])] + near, False)
    for slot, _ in far:
        arrived(slot)
    accumulate(far, False)

    n_pair = n_val * n_cond
    pos = lax.broadcasted_iota(jnp.int32, (1, n_pair), 1)
    ve_row = jnp.zeros((1, n_pair), F32)
    for v in range(n_val):
        ve_row = jnp.where(pos // n_cond == v, ve_ref[v], ve_row)
    ce_row = jnp.zeros((1, n_pair), F32)
    for c in range(n_cond):
        ce_row = jnp.where(pos % n_cond == c, ce_ref[c], ce_row)
    norm = 1.0 / math.sqrt(n_val * n_band * n_cond * n_blk)
    factor = -1.0 / (ce_row - ve_row) * norm

    ctile = 64

    def weigh(i, carry):
        rows = pl.ds(pl.multiple_of(i * ctile, ctile), ctile)
        rows_im = pl.ds(pl.multiple_of(width + i * ctile, ctile), ctile)
        a = acc[rows, :].astype(BF16).astype(F32)
        bb = acc[rows_im, :].astype(BF16).astype(F32)
        wgt[rows, 0:n_pair] = (a * factor).astype(BF16)
        wgt[rows, n_pair : 2 * n_pair] = (bb * factor).astype(BF16)
        dst_[rows, 0:n_pair] = (a - bb).astype(BF16)
        dst_[rows, n_pair : 2 * n_pair] = (a + bb).astype(BF16)
        return carry

    lax.fori_loop(0, width // ctile, weigh, 0)

    def half(blk):
        cols = pl.ds(pl.multiple_of(blk * col_block, col_block), col_block)
        return lax.dot_general(wgt[...], dst_[cols, :], NT, preferred_element_type=F32)

    theirs = half(kn)
    for i in range(n_band):
        send1[i % 2, i // 2] = theirs[i * row_block : (i + 1) * row_block, :].astype(BF16)
    first = copy(send1.at[1 - x], recv1.at[1 - x], s1_send.at[0], s1_recv.at[0], b, kn)
    second = copy(send1.at[x], recv1.at[x], s1_send.at[1], s1_recv.at[1], b, kn)
    first.start()
    second.start()
    mine = half(k)
    for i in range(n_band):
        own1[i % 2, i // 2] = mine[i * row_block : (i + 1) * row_block, :]

    first.wait_recv()
    xcopies = []
    order = sorted(range(1, nz), key=lambda t: -min(t, nz - t)) + [0]
    for t in order:
        zz = zpeer(t)
        sendx[zz] = (own1[1 - x, zz] + recv1[1 - x, zz].astype(F32)).astype(BF16)
        c = copy(sendx.at[zz], recvx.at[zz], sx_send.at[zz], sx_recv.at[zz], xn, k)
        c.start()
        xcopies.append(c)
    second.wait_recv()

    zcopies = []
    for i, t in enumerate(order):
        zz = zpeer(t)
        xcopies[i].wait_recv()
        total = own1[x, zz] + recv1[x, zz].astype(F32) + recvx[zz].astype(F32)
        if t == 0:
            final = total
        else:
            sendz[zz] = total.astype(BF16)
            c = copy(sendz.at[zz], recvz.at[z], sz_send.at[zz], sz_recv.at[z], zz * 2 + x, k)
            c.start()
            zcopies.append(c)
    for t in range(1, nz):
        zz = zpeer(t)
        copy(sendz.at[zz], recvz.at[zz], sz_send.at[zz], sz_recv.at[zz], zz * 2 + x, k).wait_recv()
        final = final + recvz[zz].astype(F32)

    packed_rows = row_block // 2
    place = lax.rem(b, per_blk)
    for j in range(per_blk):
        block = final[:, j * row_block : (j + 1) * row_block]
        sende[j] = jnp.concatenate([block[:packed_rows], block[packed_rows:]], axis=1).astype(BF16)

        @pl.when(k * per_blk + j != b)
        def _():
            copy(sende.at[j], recve.at[place], se_send.at[j], se_recv.at[place], k * per_blk + j, mirror_blk).start()

        @pl.when(k * per_blk + j == b)
        def _():
            other[j * row_block : (j + 1) * row_block, :] = block

    for j in range(per_blk):
        @pl.when(k * per_blk + j != b)
        def _():
            copy(sende.at[j], recve.at[j], se_send.at[j], se_recv.at[j], k * per_blk + j, mirror_blk).wait_recv()
            got = recve[j].astype(F32)
            other[j * row_block : j * row_block + packed_rows, :] = got[:, :row_block]
            other[j * row_block + packed_rows : (j + 1) * row_block, :] = got[:, row_block:]

    mirror = jnp.transpose(other[...])
    out_ref[0] = (final + mirror) * 0.5
    out_ref[1] = (final - mirror) * 0.5

    for c in sends + xcopies + zcopies + [first, second]:
        c.wait_send()
    for j in range(per_blk):
        @pl.when(k * per_blk + j != b)
        def _():
            copy(sende.at[j], recve.at[j], se_send.at[j], se_recv.at[j], k * per_blk + j, mirror_blk).wait_send()


def fused(valence, conduction, val_energy, cond_energy, gvectors):
    n_band = lax.axis_size("band")
    n_blk = lax.axis_size("blk")
    nz = n_band // 2
    n_val, total_points = valence.shape
    block_points, n_cond = conduction.shape
    width = gvectors.shape[1]
    row_block = width // n_band
    col_block = width // n_blk
    per_blk = col_block // row_block
    n_pair = n_val * n_cond
    dma = pltpu.SemaphoreType.DMA
    vmem = pl.BlockSpec(memory_space=pltpu.VMEM)
    return pl.pallas_call(
        functools.partial(chi_kernel, n_band, n_blk),
        out_shape=jax.ShapeDtypeStruct((2, row_block, col_block), F32),
        in_specs=[pl.BlockSpec(memory_space=pltpu.HBM)] * 5,
        out_specs=vmem,
        scratch_shapes=[
            pltpu.VMEM(valence.shape, BF16),
            pltpu.SMEM(val_energy.shape, F32),
            pltpu.SMEM(cond_energy.shape, F32),
            pltpu.VMEM(gvectors.shape, jnp.int32),
            pltpu.VMEM((8, width), F32),
            pltpu.VMEM((width, 8), F32),
            pltpu.VMEM((2, width, 128), F32),
            pltpu.VMEM((n_band, n_cond, block_points), BF16),
            pltpu.VMEM((n_band, 2 * width, block_points), BF16),
            pltpu.VMEM((nz + 1, n_pair, block_points), BF16),
            pltpu.VMEM((2 * width, n_pair), F32),
            pltpu.VMEM((width, 2 * n_pair), BF16),
            pltpu.VMEM((width, 2 * n_pair), BF16),
            pltpu.VMEM((2, nz, row_block, col_block), BF16),
            pltpu.VMEM((2, nz, row_block, col_block), F32),
            pltpu.VMEM((2, nz, row_block, col_block), BF16),
            pltpu.VMEM((nz, row_block, col_block), BF16),
            pltpu.VMEM((nz, row_block, col_block), BF16),
            pltpu.VMEM((nz, row_block, col_block), BF16),
            pltpu.VMEM((nz, row_block, col_block), BF16),
            pltpu.VMEM((per_blk, row_block // 2, 2 * row_block), BF16),
            pltpu.VMEM((per_blk, row_block // 2, 2 * row_block), BF16),
            pltpu.VMEM((col_block, row_block), F32),
            dma((5,)), dma((nz,)), dma((nz,)), dma((n_band,)), dma((2,)), dma((2,)),
            dma((nz,)), dma((nz,)), dma((nz,)), dma((nz,)), dma((per_blk,)), dma((per_blk,)),
        ],
        compiler_params=pltpu.CompilerParams(
            collective_id=0, has_side_effects=True, vmem_limit_bytes=48 * 2**20
        ),
    )(valence, conduction.T, val_energy, cond_energy, gvectors)


def table_rows(gvectors, grid, start, count):
    total_points = grid * grid * grid
    points = start + jnp.arange(count, dtype=jnp.int32)
    xs = points // (grid * grid)
    ys = points // grid % grid
    zs = points % grid
    phase_int = (
        xs[:, None] * gvectors[0][None, :]
        + ys[:, None] * gvectors[1][None, :]
        + zs[:, None] * gvectors[2][None, :]
    )
    phase_int = jnp.mod(phase_int, grid)
    phase = phase_int.astype(jnp.float32) * (2.0 * math.pi / grid)
    scale = 1.0 / math.sqrt(total_points)
    return jnp.concatenate([jnp.cos(phase) * scale, -jnp.sin(phase) * scale], axis=1).astype(
        jnp.bfloat16
    )


def chi_part(weighted, elements, width, row_start, row_count, col_start, col_count):
    dims = (((0,), (0,)), ((), ()))
    left_re = lax.dynamic_slice_in_dim(weighted, row_start, row_count, 1)
    left_im = lax.dynamic_slice_in_dim(weighted, row_start + width, row_count, 1)
    right_re = lax.dynamic_slice_in_dim(elements, col_start, col_count, 1)
    right_im = lax.dynamic_slice_in_dim(elements, col_start + width, col_count, 1)
    real_part = lax.dot_general(
        left_re, right_re, dims, preferred_element_type=jnp.float32
    ) + lax.dot_general(left_im, right_im, dims, preferred_element_type=jnp.float32)
    imag_part = lax.dot_general(
        left_im, right_re, dims, preferred_element_type=jnp.float32
    ) - lax.dot_general(left_re, right_im, dims, preferred_element_type=jnp.float32)
    return (real_part, imag_part)


def per_device(valence, conduction, val_energy, cond_energy, gvectors):
    width = gvectors.shape[1]
    val_count = valence.shape[0]
    cond_count = conduction.shape[1]
    n_band = lax.axis_size("band")
    n_blk = lax.axis_size("blk")
    row_block = width // n_band
    col_block = width // n_blk
    points_all = valence.shape[1]
    point_block = min(512, points_all)
    gathered = lax.all_gather(conduction, "band", axis=0, tiled=True)
    cond_rows = jnp.transpose(gathered).astype(jnp.float32)
    summed = jnp.zeros((val_count * cond_count, 2 * width), jnp.float32)
    for block_index in range(points_all // point_block):
        start = block_index * point_block
        vals = valence[:, start : start + point_block].astype(jnp.float32)
        conds = cond_rows[:, start : start + point_block]
        pair = (vals[:, None, :] * conds[None, :, :]).astype(jnp.bfloat16).reshape(-1, point_block)
        tab_block = table_rows(gvectors, GRID, start, point_block)
        summed = summed + jnp.dot(pair, tab_block, preferred_element_type=jnp.float32)
    elements = summed.astype(jnp.bfloat16)
    val_total = val_count * n_band
    cond_total = cond_count * n_blk
    norm = 1.0 / math.sqrt(val_total * cond_total)
    factor = (-1.0 / (cond_energy[None, :] - val_energy[:, None]) * norm).reshape(-1, 1)
    weighted = (elements.astype(jnp.float32) * factor).astype(jnp.bfloat16)
    band_index = lax.axis_index("band")
    blk_index = lax.axis_index("blk")
    real_part, imag_part = chi_part(weighted, elements, width, 0, width, 0, width)
    total = lax.psum(jnp.stack([real_part, imag_part]), ("band", "blk"))
    mine = lax.dynamic_slice_in_dim(total, band_index * row_block, row_block, 1)
    return lax.dynamic_slice_in_dim(mine, blk_index * col_block, col_block, 2)


def fits(mesh, valence, conduction, gvectors):
    n_band, n_blk, parts = mesh.shape["band"], mesh.shape["blk"], mesh.shape["groups"]
    width = gvectors.shape[1] // parts
    return (
        n_blk == 2 and n_band % 2 == 0 and n_band <= 16 and n_band % n_blk == 0
        and width // n_band == 64 and valence.shape[1] == GRID**3
        and conduction.shape[0] // n_band % (GRID * GRID) == 0
        and conduction.shape[1] // (parts * n_blk) % 16 == 0
    )


def solution(mesh):
    in_specs = (
        P(("groups", "band"), None),
        P("band", ("groups", "blk")),
        P(("groups", "band")),
        P(("groups", "blk")),
        P(None, "groups"),
    )
    out_specs = P(None, ("groups", "band"), "blk")

    def run(valence, conduction, val_energy, cond_energy, gvectors):
        body = fused if fits(mesh, valence, conduction, gvectors) else per_device
        return jax.shard_map(
            body, mesh=mesh, in_specs=in_specs, out_specs=out_specs, check_vma=False
        )(valence, conduction, val_energy, cond_energy, gvectors)

    return run
```
